256 devices in a mesh: gx: 8 (over z), gy: 8 (over y, core), gz: 4 (over x).
Axes of the slice: x: 4, y: 4, z: 8, core: 2. Of those that a mesh axis runs over, the one named last changes fastest.
Arguments:
- particle_vel: float32 [3, 256, 32, 256], P(None, ('gx', 'gy', 'gz')), may hold values from -6 to 6
- drag_coef: float32 [256, 32, 256], P(('gx', 'gy', 'gz')), may hold values from 1 to 8
- volume: float32 [256, 32, 256], P(('gx', 'gy', 'gz')), may hold values from 0.2 to 3
- stencil_weight: float32 [256, 32, 256], P(('gx', 'gy', 'gz')), may hold values from 0 to 1
- cell_index: int32 [256, 32, 256], P(('gx', 'gy', 'gz')), may hold values from 0 to 131070, as said below
- send_counts: int32 [256, 32], P(('gx', 'gy', 'gz')), may hold values from 1 to 256, as said below
- background_momentum: float32 [3, 256, 256, 512], P(None, 'gx', 'gy', 'gz'), may hold values from -6 to 6
Outputs:
- pressure: float32 [256, 256, 512], P('gx', 'gy', 'gz')
- slot_velocity: float32 [3, 256, 32, 256], P(None, ('gx', 'gy', 'gz'))
The draws below stay inside these ranges and needn't reach their ends.
Inputs may be any that keep to these rules, and one draw needn't show every extreme that they name: The z coordinate of every cell_index within its block is at most 126, so both stencil cells lie in the destination device's block. `send_counts`: slots of a row below its count are live, the rest empty. Every device holds 256 live slots for its own fluid block, and in every draw some destination device receives 256 live slots from every device of its gx plane.
All inputs are finite; a program needn't handle non-finite values.
Results may differ from the reference program's by a relative error of at most 0.0003.
Values sent between devices are 32-bit elements; how exact they have to be, the bound alone decides.
A program may use at most 64 MiB of HBM per device.

```python
import math
import jax
import jax.numpy as jnp

CX = 32
CY = 32
CZ = 128
CAP = 256
SWEEPS = 4
GROUP = 32
NX = 256
NY = 256
NZ = 512
N_GX = 8
N_GY = 8
N_GZ = 4
DEVICES = 256


def draw_cell_index(key, part):
    drawn_ids = jax.random.randint(key, (DEVICES, GROUP, CAP), 0, CX * CY * (CZ - 1))
    column = drawn_ids // (CZ - 1)
    height = drawn_ids % (CZ - 1)
    flat_cells = column * CZ + height
    return flat_cells.at[0, 0, 0].set(CX * CY * CZ - 2).astype(jnp.int32)


def draw_send_counts(key, part):
    jitter_key = jax.random.fold_in(key, 7)
    rate_key = jax.random.fold_in(key, 11)
    boost_key = jax.random.fold_in(key, 13)
    boost_count_key = jax.random.fold_in(key, 17)
    heavy_key = jax.random.fold_in(key, 19)
    sources = jnp.arange(DEVICES, dtype=jnp.int32)
    targets = jnp.arange(GROUP, dtype=jnp.int32)
    src_y = sources % GROUP // N_GZ
    src_z = sources % N_GZ
    dst_y = targets // N_GZ
    dst_z = targets % N_GZ
    step_y = jnp.abs(src_y[:, None] - dst_y[None, :])
    step_y = jnp.minimum(step_y, N_GY - step_y)
    step_z = jnp.abs(src_z[:, None] - dst_z[None, :])
    step_z = jnp.minimum(step_z, N_GZ - step_z)
    distance = step_y + step_z
    rate_pct = jax.random.randint(rate_key, (DEVICES, 1), 45, 76)
    factor = jnp.full((DEVICES, GROUP), 1000000, dtype=jnp.int32)
    for level in range(12):
        factor = jnp.where(distance > level, factor // 100 * rate_pct, factor)
    jitter = jax.random.randint(jitter_key, (DEVICES, GROUP), 700, 1001)
    counts = jnp.maximum(1, CAP * (factor // 1000) * jitter // 1000000)
    boosted = jax.random.randint(boost_key, (DEVICES, GROUP), 0, 8) == 0
    boost_counts = jax.random.randint(boost_count_key, (DEVICES, GROUP), 1, CAP + 1)
    counts = jnp.where(boosted, boost_counts, counts)
    counts = jnp.where(distance == 0, CAP, counts)
    heavy_target = jax.random.randint(heavy_key, (N_GX,), 0, GROUP)
    heavy = targets[None, :] == heavy_target[sources // GROUP][:, None]
    counts = jnp.where(heavy, CAP, counts)
    return jnp.clip(counts, 1, CAP).astype(jnp.int32)


def level_of(stream_key, dims, cuts, smallest, high):
    loudness = 1.0
    for dim, parts in cuts:
        draws = jax.random.uniform(jax.random.fold_in(jax.random.fold_in(stream_key, 6), dim), (parts,), jnp.float32, smallest / len(cuts), high / len(cuts))
        loudness = loudness * jnp.repeat(jnp.exp(draws), dims[dim] // parts).reshape((-1,) + (1,) * (len(dims) - 1 - dim))
    return loudness


def scatter_about(stream_key, dims, spread, limit, split=(), kind=jnp.bfloat16):
    loudness = level_of(stream_key, dims, split, -0.22, 0.18) if split else 1.0
    entries = jax.random.normal(stream_key, dims, jnp.float32) * spread * loudness
    return jnp.minimum(jnp.maximum(entries, -limit), limit).astype(kind)


def setup_inputs(seed: int = 0) -> dict:
    streams_of = jax.random.split(jax.random.key(seed), 8)
    return {
        "particle_vel": scatter_about(streams_of[0], (3, DEVICES, GROUP, CAP), 1.0, 6.0, ((1, 256),), jnp.float32),
        "drag_coef": jnp.clip(jnp.exp(math.log(8.0) - 2.0794415 * jax.random.uniform(streams_of[1], (DEVICES, GROUP, CAP), jnp.float32) ** level_of(streams_of[1], (DEVICES, GROUP, CAP), ((0, 256),), -0.2, 0.2)), 1.0, 8.0),
        "volume": jnp.clip(jnp.exp(math.log(3.0) - 2.7080502 * jax.random.uniform(streams_of[2], (DEVICES, GROUP, CAP), jnp.float32) ** level_of(streams_of[2], (DEVICES, GROUP, CAP), ((0, 256),), -0.2, 0.2)), 0.2, 3.0),
        "stencil_weight": jnp.clip(1.0 * jax.random.uniform(streams_of[3], (DEVICES, GROUP, CAP), jnp.float32) ** level_of(streams_of[3], (DEVICES, GROUP, CAP), ((0, 256),), -0.2, 0.2), 0.0, 1.0),
        "cell_index": draw_cell_index(jax.random.fold_in(streams_of[7], 71), 0),
        "send_counts": draw_send_counts(jax.random.fold_in(streams_of[7], 71), 0),
        "background_momentum": scatter_about(streams_of[6], (3, NX, NY, NZ), 1.0, 6.0, ((1, 8), (2, 8), (3, 4)), jnp.float32),
    }


def neighbour_total(padded, weights):
    plus_x, minus_x, plus_y, minus_y, plus_z, minus_z = weights
    total = plus_x * padded[2:, 1:-1, 1:-1] + minus_x * padded[:-2, 1:-1, 1:-1]
    total = total + plus_y * padded[1:-1, 2:, 1:-1] + minus_y * padded[1:-1, :-2, 1:-1]
    return total + plus_z * padded[1:-1, 1:-1, 2:] + minus_z * padded[1:-1, 1:-1, :-2]


def face_weights(porous):
    centre = porous[1:-1, 1:-1, 1:-1]
    weights = (0.5 * (centre + porous[2:, 1:-1, 1:-1]), 0.5 * (centre + porous[:-2, 1:-1, 1:-1]),
               0.5 * (centre + porous[1:-1, 2:, 1:-1]), 0.5 * (centre + porous[1:-1, :-2, 1:-1]),
               0.5 * (centre + porous[1:-1, 1:-1, 2:]), 0.5 * (centre + porous[1:-1, 1:-1, :-2]))
    diagonal = weights[0] + weights[1] + weights[2] + weights[3] + weights[4] + weights[5]
    return weights, diagonal


def divergence(moment):
    total = 0.5 * (moment[0, 2:, 1:-1, 1:-1] - moment[0, :-2, 1:-1, 1:-1])
    total = total + 0.5 * (moment[1, 1:-1, 2:, 1:-1] - moment[1, 1:-1, :-2, 1:-1])
    return total + 0.5 * (moment[2, 1:-1, 1:-1, 2:] - moment[2, 1:-1, 1:-1, :-2])


def gradient_of(padded):
    return jnp.stack([0.5 * (padded[2:, 1:-1, 1:-1] - padded[:-2, 1:-1, 1:-1]),
                      0.5 * (padded[1:-1, 2:, 1:-1] - padded[1:-1, :-2, 1:-1]),
                      0.5 * (padded[1:-1, 1:-1, 2:] - padded[1:-1, 1:-1, :-2])])


def reference(particle_vel, drag_coef, volume, stencil_weight, cell_index, send_counts, background_momentum):
    device_count, group_size, capacity = drag_coef.shape
    block_cells = CX * CY * CZ
    slot_pos = jnp.arange(capacity, dtype=jnp.int32)
    alive = (slot_pos[None, None, :] < send_counts[:, :, None]).astype(jnp.float32)
    strength = drag_coef * alive
    carried = jnp.stack([strength * particle_vel[0], strength * particle_vel[1],
                         strength * particle_vel[2], volume * alive]).reshape(4, -1)
    source = jnp.arange(device_count, dtype=jnp.int32)
    target = (source // group_size * group_size)[:, None] + jnp.arange(group_size, dtype=jnp.int32)[None, :]
    flat_ids = (target[:, :, None] * block_cells + cell_index).reshape(-1).astype(jnp.int32)
    share = stencil_weight.reshape(-1)
    deposited = jnp.zeros((4, device_count * block_cells), jnp.float32)
    deposited = deposited.at[:, flat_ids].add(carried * share)
    deposited = deposited.at[:, flat_ids + 1].add(carried * (1.0 - share))
    deposited = deposited.reshape(4, N_GX, N_GY, N_GZ, CX, CY, CZ).transpose(0, 1, 4, 2, 5, 3, 6).reshape(4, NX, NY, NZ)
    momentum = background_momentum + deposited[:3]
    porosity = 1.0 / (1.0 + deposited[3])
    weights, diagonal = face_weights(jnp.pad(porosity, 1, constant_values=1.0))
    source_div = divergence(jnp.pad(momentum, ((0, 0), (1, 1), (1, 1), (1, 1))))
    pressure = jnp.zeros((NX, NY, NZ), jnp.float32)
    for sweep_no in range(SWEEPS):
        pressure = (neighbour_total(jnp.pad(pressure, 1), weights) - source_div) / diagonal
    fluid_velocity = porosity[None] * (momentum - gradient_of(jnp.pad(pressure, 1)))
    velocity_blocks = fluid_velocity.reshape(3, N_GX, CX, N_GY, CY, N_GZ, CZ).transpose(0, 1, 3, 5, 2, 4, 6).reshape(3, -1)
    picked = share * velocity_blocks[:, flat_ids] + (1.0 - share) * velocity_blocks[:, flat_ids + 1]
    slot_velocity = picked.reshape(3, device_count, group_size, capacity) * alive[None]
    return pressure, slot_velocity
```

```python
import functools

import jax
import jax.numpy as jnp
from jax import lax
from jax.experimental import pallas as pl
from jax.experimental.pallas import tpu as pltpu
from jax.sharding import PartitionSpec as P

SWEEPS = 4
F32 = jnp.float32
BF16 = jnp.bfloat16
MESH = pl.DeviceIdType.MESH
LANES = 128
STEP = 4


def iota(shape, dim):
    return lax.broadcasted_iota(jnp.int32, shape, dim)


def dot(lhs, rhs, contract):
    return lax.dot_general(lhs, rhs, (contract, ((), ())), preferred_element_type=F32)


def split(value):
    high = value.astype(BF16)
    return high.astype(F32), value - high.astype(F32)


def step_kernel(
    sizes,
    vel_ref, drag_ref, vol_ref, weight_ref, cell_ref, counts_ref, back_hbm,
    pressure_ref, slots_ref,
    back, payload, arrived, total, mom_x, mom_y, mom_z, porous, coef, press,
    vel_t, picked, returned,
    face_xs, face_xr, face_ys, face_yr, face_zs, face_zr,
    back_sem, pay_ssem, pay_rsem, ret_ssem, ret_rsem, halo_ssem, halo_rsem,
):
    n_x, n_y, n_z = sizes
    group = n_y * n_z
    capacity = drag_ref.shape[2]
    size_x, size_y, size_z = pressure_ref.shape
    columns = size_x * size_y
    per_tile = LANES // size_y
    tiles = size_x // per_tile
    at_x, at_y, at_z = lax.axis_index("gx"), lax.axis_index("gy"), lax.axis_index("gz")
    me = at_y * n_z + at_z

    def place(offset):
        there_y = lax.rem(at_y + offset // n_z, n_y)
        there_z = lax.rem(at_z + lax.rem(offset, n_z), n_z)
        return there_y, there_z

    def place_back(offset):
        there_y = lax.rem(at_y - offset // n_z + n_y, n_y)
        there_z = lax.rem(at_z - lax.rem(offset, n_z) + n_z, n_z)
        return there_y, there_z

    x_down = (lax.rem(at_x + n_x - 1, n_x), at_y, at_z)
    x_up = (lax.rem(at_x + 1, n_x), at_y, at_z)
    y_down = (at_x, lax.rem(at_y + n_y - 1, n_y), at_z)
    y_up = (at_x, lax.rem(at_y + 1, n_y), at_z)
    z_down = (at_x, at_y, lax.rem(at_z + n_z - 1, n_z))
    z_up = (at_x, at_y, lax.rem(at_z + 1, n_z))

    barrier = pltpu.get_barrier_semaphore()

    def greet(offset, carry):
        there_y, there_z = place(offset)
        pl.semaphore_signal(barrier, inc=1, device_id=(at_x, there_y, there_z), device_id_type=MESH)
        return carry

    lax.fori_loop(1, group, greet, 0)
    for there in (x_down, x_up):
        pl.semaphore_signal(barrier, inc=1, device_id=there, device_id_type=MESH)

    back_copy = pltpu.make_async_copy(back_hbm, back, back_sem)
    back_copy.start()

    eye = iota((group, group), 0) == iota((group, group), 1)
    counts = jnp.broadcast_to(counts_ref[...].astype(F32), (group, group))
    counts = jnp.sum(jnp.where(eye, counts, 0.0), axis=1, keepdims=True)
    alive = (iota((group, capacity), 1).astype(F32) < counts).astype(F32)
    strength = drag_ref[0] * alive
    cell = cell_ref[0]
    rows = [strength * vel_ref[k, 0] for k in range(3)]
    rows.append(vol_ref[0] * alive)
    rows.append(weight_ref[0])
    rows.append(lax.rem(cell, size_z).astype(F32))
    rows.append(lax.div(cell, size_z).astype(F32))
    for k, row in enumerate(rows):
        payload[:, k, :] = row
    payload[:, 7, :] = rows[6]

    pl.semaphore_wait(barrier, group + 1)

    def payload_copy(offset):
        there_y, there_z = place(offset)
        return pltpu.make_async_remote_copy(
            src_ref=payload.at[there_y * n_z + there_z],
            dst_ref=arrived.at[offset],
            send_sem=pay_ssem.at[offset],
            recv_sem=pay_rsem.at[offset],
            device_id=(at_x, there_y, there_z),
            device_id_type=MESH,
        )

    def send_payload(offset, carry):
        payload_copy(offset).start()
        return carry

    lax.fori_loop(1, group, send_payload, 0)
    arrived[0] = payload[me]
    total[...] = jnp.zeros_like(total)

    width = STEP * capacity

    def chunk_rows(step):
        return jnp.concatenate([arrived[step * STEP + i] for i in range(STEP)], axis=1)

    def column_hot(slots):
        return (iota((columns, width), 0).astype(F32) == slots[6:7]).astype(F32).astype(BF16)

    def deposit(step, carry):
        for i in range(STEP):
            offset = step * STEP + i

            @pl.when(offset > 0)
            def _():
                payload_copy(offset).wait_recv()

        slots = chunk_rows(step)
        hot = column_hot(slots)
        level = iota((size_z, width), 0).astype(F32)
        here = level == slots[5:6]
        above = level == slots[5:6] + 1.0
        share = slots[4:5]
        highs, lows = [], []
        for k in range(4):
            first = split(slots[k : k + 1] * share)
            second = split(slots[k : k + 1] * (1.0 - share))
            for parts, a, b in ((highs, first[0], second[0]), (lows, first[1], second[1])):
                parts.append(jnp.where(here, a, jnp.where(above, b, 0.0)).astype(BF16))
        spread_high = jnp.concatenate(highs, axis=0)
        spread_low = jnp.concatenate(lows, axis=0)
        total[...] += dot(hot, spread_high, ((1,), (1,))) + dot(hot, spread_low, ((1,), (1,)))
        return carry

    lax.fori_loop(0, group // STEP, deposit, 0)

    def halo_copies(exchange, slot, fields):
        copies = []
        for axis, (sends, receives, down, up) in enumerate(
            (
                (face_xs, face_xr, x_down, x_up),
                (face_ys, face_yr, y_down, y_up),
                (face_zs, face_zr, z_down, z_up),
            )
        ):
            for side, there in ((0, down), (1, up)):
                copies.append(
                    pltpu.make_async_remote_copy(
                        src_ref=sends.at[side, pl.ds(slot, fields)],
                        dst_ref=receives.at[1 - side, pl.ds(slot, fields)],
                        send_sem=halo_ssem.at[exchange, 2 * axis + side],
                        recv_sem=halo_rsem.at[exchange, 2 * axis + 1 - side],
                        device_id=there,
                        device_id_type=MESH,
                    )
                )
        return copies

    def start_halos(exchange, slot, fields):
        for copy in halo_copies(exchange, slot, fields):
            copy.start()

    def wait_halos(exchange, slot, fields):
        for copy in halo_copies(exchange, slot, fields):
            copy.wait_recv()

    inside = [
        jnp.where(flag, 1.0, 0.0)
        for flag in (at_x > 0, at_x < n_x - 1, at_y > 0, at_y < n_y - 1, at_z > 0, at_z < n_z - 1)
    ]
    row_of = iota((size_y, size_z), 0)
    lane_of = iota((size_y, size_z), 1)
    diagonals = [lane_of == row_of + j * size_y for j in range(per_tile)]
    first_row, last_row = row_of == 0, row_of == size_y - 1
    first_lane, last_lane = lane_of == 0, lane_of == size_z - 1

    def put_y(slot, x, plane):
        face_ys[0, slot, pl.ds(x, 1), :] = plane[:1]
        face_ys[1, slot, pl.ds(x, 1), :] = plane[size_y - 1 :]

    def put_z(slot, tile, planes):
        for side, lane in ((0, 0), (1, size_z - 1)):
            gathered = 0.0
            for j, plane in enumerate(planes):
                gathered = gathered + jnp.where(diagonals[j], plane[:, lane : lane + 1], 0.0)
            face_zs[side, slot, pl.ds(tile, 1), :] = jnp.sum(gathered, axis=0, keepdims=True)

    def y_low(slot, x):
        return face_yr[0, slot, pl.ds(x, 1), :] * inside[2]

    def y_high(slot, x):
        return face_yr[1, slot, pl.ds(x, 1), :] * inside[3]

    def z_side(side, slot, tile, j):
        row = face_zr[side, slot, pl.ds(tile, 1), :] * inside[4 + side]
        return jnp.sum(jnp.where(diagonals[j], row, 0.0), axis=1, keepdims=True)

    def y_pair(plane, low, high):
        before = jnp.where(first_row, low, pltpu.roll(plane, 1, 0))
        after = jnp.where(last_row, high, pltpu.roll(plane, size_y - 1, 0))
        return before, after

    def z_pair(plane, low, high):
        before = jnp.where(first_lane, low, pltpu.roll(plane, 1, 1))
        after = jnp.where(last_lane, high, pltpu.roll(plane, size_z - 1, 1))
        return before, after

    def tile_rows(tile):
        return pl.ds(pl.multiple_of(tile * LANES, LANES), LANES)

    back_copy.wait()

    def fields_step(tile, carry):
        block = total[tile_rows(tile), :]
        heights = [[], []]
        for j in range(per_tile):
            x = tile * per_tile + j
            part = block[j * size_y : (j + 1) * size_y]
            along = [back[k, x] + part[:, k * size_z : (k + 1) * size_z] for k in range(3)]
            solid = part[:, 3 * size_z :]
            mom_x[x + 1] = along[0]
            mom_y[x] = along[1]
            mom_z[x] = along[2]
            porous[x + 1] = solid
            put_y(0, x, along[1])
            put_y(1, x, solid)
            heights[0].append(along[2])
            heights[1].append(solid)
        put_z(0, tile, heights[0])
        put_z(1, tile, heights[1])
        return carry

    lax.fori_loop(0, tiles, fields_step, 0)
    for side, x in ((0, 1), (1, size_x)):
        face_xs[side, 0] = mom_x[x]
        face_xs[side, 1] = porous[x]
    start_halos(0, 0, 2)

    def porosity_step(tile, carry):
        for j in range(per_tile):
            x = tile * per_tile + j + 1
            porous[x] = 1.0 / (1.0 + porous[x])
        return carry

    lax.fori_loop(0, tiles, porosity_step, 0)
    wait_halos(0, 0, 2)
    for side, x in ((0, 0), (1, size_x + 1)):
        mom_x[x] = face_xr[side, 0] * inside[side]
        porous[x] = 1.0 / (1.0 + face_xr[side, 1] * inside[side])

    def put_pressure(slot, tile, x, planes, buffer):
        for j, plane in enumerate(planes):
            press[buffer, x + j + 1] = plane
            put_y(slot, x + j, plane)
        put_z(slot, tile, planes)

    def send_pressure(exchange, buffer):
        slot = exchange + 1
        for side, x in ((0, 1), (1, size_x)):
            face_xs[side, slot] = press[buffer, x]
        start_halos(exchange, slot, 1)

    def take_pressure(exchange, buffer):
        slot = exchange + 1
        wait_halos(exchange, slot, 1)
        for side, x in ((0, 0), (1, size_x + 1)):
            press[buffer, x] = face_xr[side, slot] * inside[side]

    def weights_step(tile, carry):
        planes = []
        for j in range(per_tile):
            x = tile * per_tile + j
            centre = porous[x + 1]
            around = [porous[x + 2], porous[x]]
            low, high = y_pair(centre, 1.0 / (1.0 + y_low(1, x)), 1.0 / (1.0 + y_high(1, x)))
            around += [high, low]
            low, high = z_pair(
                centre,
                1.0 / (1.0 + z_side(0, 1, tile, j)),
                1.0 / (1.0 + z_side(1, 1, tile, j)),
            )
            around += [high, low]
            faces = [0.5 * (centre + other) for other in around]
            diagonal = faces[0] + faces[1] + faces[2] + faces[3] + faces[4] + faces[5]
            inverse = 1.0 / diagonal
            low, high = y_pair(mom_y[x], y_low(0, x), y_high(0, x))
            source = (mom_x[x + 2] - mom_x[x]) + (high - low)
            low, high = z_pair(mom_z[x], z_side(0, 0, tile, j), z_side(1, 0, tile, j))
            source = 0.5 * (source + (high - low))
            for k in range(6):
                coef[k, x] = faces[k] * inverse
            scaled = source * inverse
            coef[6, x] = scaled
            planes.append(-scaled)
        put_pressure(2, tile, tile * per_tile, planes, 1)
        return carry

    lax.fori_loop(0, tiles, weights_step, 0)
    send_pressure(1, 1)

    def sweep(exchange, carry):
        buffer = lax.rem(exchange, 2)
        take_pressure(exchange, buffer)
        slot = exchange + 1

        def sweep_step(tile, inner):
            planes = []
            for j in range(per_tile):
                x = tile * per_tile + j
                centre = press[buffer, x + 1]
                new = coef[0, x] * press[buffer, x + 2] + coef[1, x] * press[buffer, x]
                low, high = y_pair(centre, y_low(slot, x), y_high(slot, x))
                new = new + coef[2, x] * high + coef[3, x] * low
                low, high = z_pair(
                    centre, z_side(0, slot, tile, j), z_side(1, slot, tile, j)
                )
                new = new + coef[4, x] * high + coef[5, x] * low
                planes.append(new - coef[6, x])
            put_pressure(slot + 1, tile, tile * per_tile, planes, 1 - buffer)
            return inner

        lax.fori_loop(0, tiles, sweep_step, 0)
        send_pressure(exchange + 1, 1 - buffer)
        return carry

    lax.fori_loop(1, SWEEPS, sweep, 0)

    last = SWEEPS % 2
    take_pressure(SWEEPS, last)

    def velocity_step(tile, carry):
        parts = [[], [], []]
        for j in range(per_tile):
            x = tile * per_tile + j
            centre = press[last, x + 1]
            pressure_ref[x] = centre
            hollow = porous[x + 1]
            slope = press[last, x + 2] - press[last, x]
            parts[0].append(hollow * (mom_x[x + 1] - 0.5 * slope))
            low, high = y_pair(centre, y_low(SWEEPS + 1, x), y_high(SWEEPS + 1, x))
            parts[1].append(hollow * (mom_y[x] - 0.5 * (high - low)))
            low, high = z_pair(
                centre, z_side(0, SWEEPS + 1, tile, j), z_side(1, SWEEPS + 1, tile, j)
            )
            parts[2].append(hollow * (mom_z[x] - 0.5 * (high - low)))
        for k in range(3):
            turned = jnp.concatenate(parts[k], axis=0).T
            high, low = split(turned)
            vel_t[k * size_z : (k + 1) * size_z, tile_rows(tile)] = high.astype(BF16)
            vel_t[(3 + k) * size_z : (4 + k) * size_z, tile_rows(tile)] = low.astype(BF16)
        return carry

    lax.fori_loop(0, tiles, velocity_step, 0)

    def return_copy(offset):
        there_y, there_z = place_back(offset)
        return pltpu.make_async_remote_copy(
            src_ref=picked.at[offset],
            dst_ref=returned.at[me],
            send_sem=ret_ssem.at[offset],
            recv_sem=ret_rsem.at[offset],
            device_id=(at_x, there_y, there_z),
            device_id_type=MESH,
        )

    def pick(turn, carry):
        step = group // STEP - 1 - turn
        slots = chunk_rows(step)
        both = dot(vel_t[...], column_hot(slots), ((1,), (0,)))
        level = iota((size_z, width), 0).astype(F32)
        share = slots[4:5]
        reach = jnp.where(
            level == slots[5:6], share, jnp.where(level == slots[5:6] + 1.0, 1.0 - share, 0.0)
        )
        found = []
        for k in range(3):
            value = (
                both[k * size_z : (k + 1) * size_z] + both[(3 + k) * size_z : (4 + k) * size_z]
            )
            found.append(jnp.sum(value * reach, axis=0, keepdims=True))
        found.append(jnp.zeros_like(found[0]))
        found = jnp.concatenate(found, axis=0)
        for i in range(STEP):
            offset = step * STEP + i
            picked[offset] = found[:, i * capacity : (i + 1) * capacity]

            @pl.when(offset > 0)
            def _():
                return_copy(offset).start()

        return carry

    lax.fori_loop(0, group // STEP, pick, 0)
    returned[me] = picked[0]

    def finish(offset, carry):
        copy = return_copy(offset)
        copy.wait_recv()
        copy.wait_send()
        payload_copy(offset).wait_send()
        return carry

    lax.fori_loop(1, group, finish, 0)
    for k in range(3):
        slots_ref[k, 0] = returned[:, k, :] * alive

    def finish_halos(exchange, carry):
        for copy in halo_copies(exchange, exchange + 1, 1):
            copy.wait_send()
        return carry

    for copy in halo_copies(0, 0, 2):
        copy.wait_send()
    lax.fori_loop(1, SWEEPS + 1, finish_halos, 0)


def per_device(sizes, *args):
    vel, drag = args[0], args[1]
    back = args[6]
    group, capacity = drag.shape[1:]
    _, size_x, size_y, size_z = back.shape
    columns = size_x * size_y
    tile_rows = columns // LANES
    slots = SWEEPS + 2
    vmem = pl.BlockSpec(memory_space=pltpu.VMEM)
    field = pltpu.VMEM((size_x, size_y, size_z), F32)
    padded = pltpu.VMEM((size_x + 2, size_y, size_z), F32)
    dma = pltpu.SemaphoreType.DMA
    return pl.pallas_call(
        functools.partial(step_kernel, sizes),
        out_shape=(
            jax.ShapeDtypeStruct((size_x, size_y, size_z), F32),
            jax.ShapeDtypeStruct(vel.shape, F32),
        ),
        in_specs=[vmem] * 6 + [pl.BlockSpec(memory_space=pl.ANY)],
        out_specs=(vmem, vmem),
        scratch_shapes=[
            pltpu.VMEM(back.shape, F32),
            pltpu.VMEM((group, 8, capacity), F32),
            pltpu.VMEM((group, 8, capacity), F32),
            pltpu.VMEM((columns, 4 * size_z), F32),
            padded,
            field,
            field,
            padded,
            pltpu.VMEM((7, size_x, size_y, size_z), F32),
            pltpu.VMEM((2, size_x + 2, size_y, size_z), F32),
            pltpu.VMEM((6 * size_z, columns), BF16),
            pltpu.VMEM((group, 4, capacity), F32),
            pltpu.VMEM((group, 4, capacity), F32),
            pltpu.VMEM((2, slots, size_y, size_z), F32),
            pltpu.VMEM((2, slots, size_y, size_z), F32),
            pltpu.VMEM((2, slots, size_x, size_z), F32),
            pltpu.VMEM((2, slots, size_x, size_z), F32),
            pltpu.VMEM((2, slots, tile_rows, LANES), F32),
            pltpu.VMEM((2, slots, tile_rows, LANES), F32),
            dma,
            dma((group,)),
            dma((group,)),
            dma((group,)),
            dma((group,)),
            dma((SWEEPS + 1, 6)),
            dma((SWEEPS + 1, 6)),
        ],
        compiler_params=pltpu.CompilerParams(
            collective_id=0, has_side_effects=True, vmem_limit_bytes=56 * 2**20
        ),
    )(*args)


def solution(mesh):
    sizes = (mesh.shape["gx"], mesh.shape["gy"], mesh.shape["gz"])
    block = ("gx", "gy", "gz")
    return jax.shard_map(
        functools.partial(per_device, sizes),
        mesh=mesh,
        in_specs=(
            P(None, block, None, None),
            P(block, None, None),
            P(block, None, None),
            P(block, None, None),
            P(block, None, None),
            P(block, None),
            P(None, *block),
        ),
        out_specs=(P(*block), P(None, block, None, None)),
        check_vma=False,
    )
```

```python
import functools

import jax
import jax.numpy as jnp
from jax import lax
from jax.experimental import pallas as pl
from jax.experimental.pallas import tpu as pltpu
from jax.sharding import PartitionSpec as P

SWEEPS = 4
F32 = jnp.float32
BF16 = jnp.bfloat16
MESH = pl.DeviceIdType.MESH
LANES = 128
STEP = 4
UNROLL = 4


def iota(shape, dim):
    return lax.broadcasted_iota(jnp.int32, shape, dim)


def dot(lhs, rhs, contract):
    return lax.dot_general(lhs, rhs, (contract, ((), ())), preferred_element_type=F32)


def split(value):
    high = value.astype(BF16)
    return high.astype(F32), value - high.astype(F32)


def step_kernel(
    sizes,
    vel_ref, drag_ref, vol_ref, weight_ref, cell_ref, counts_ref, back_hbm,
    pressure_ref, slots_ref,
    back, payload, arrived, total, mom_x, mom_y, mom_z, porous, coef, press,
    diagonal, edge_x, edge_y, edge_z, work_z, edge_v, vel_t, picked, returned,
    face_xs, face_xr, face_ys, face_yr, face_zs, face_zr,
    back_sem, pay_ssem, pay_rsem, ret_ssem, ret_rsem, halo_ssem, halo_rsem,
):
    n_x, n_y, n_z = sizes
    group = n_y * n_z
    capacity = drag_ref.shape[2]
    columns, size_z = pressure_ref.shape
    size_y = face_xs.shape[2]
    size_x = columns // size_y
    per_tile = LANES // size_y
    tiles = size_x // per_tile
    at_x, at_y, at_z = lax.axis_index("gx"), lax.axis_index("gy"), lax.axis_index("gz")
    me = at_y * n_z + at_z

    def place(offset):
        there_y = lax.rem(at_y + offset // n_z, n_y)
        there_z = lax.rem(at_z + lax.rem(offset, n_z), n_z)
        return there_y, there_z

    def place_back(offset):
        there_y = lax.rem(at_y - offset // n_z + n_y, n_y)
        there_z = lax.rem(at_z - lax.rem(offset, n_z) + n_z, n_z)
        return there_y, there_z

    x_down = (lax.rem(at_x + n_x - 1, n_x), at_y, at_z)
    x_up = (lax.rem(at_x + 1, n_x), at_y, at_z)
    y_down = (at_x, lax.rem(at_y + n_y - 1, n_y), at_z)
    y_up = (at_x, lax.rem(at_y + 1, n_y), at_z)
    z_down = (at_x, at_y, lax.rem(at_z + n_z - 1, n_z))
    z_up = (at_x, at_y, lax.rem(at_z + 1, n_z))

    barrier = pltpu.get_barrier_semaphore()

    def greet(offset, carry):
        there_y, there_z = place(offset)
        pl.semaphore_signal(barrier, inc=1, device_id=(at_x, there_y, there_z), device_id_type=MESH)
        return carry

    lax.fori_loop(1, group, greet, 0)
    for there in (x_down, x_up):
        pl.semaphore_signal(barrier, inc=1, device_id=there, device_id_type=MESH)

    back_copy = pltpu.make_async_copy(back_hbm, back, back_sem)
    back_copy.start()

    eye = iota((group, group), 0) == iota((group, group), 1)
    counts = jnp.broadcast_to(counts_ref[...].astype(F32), (group, group))
    counts = jnp.sum(jnp.where(eye, counts, 0.0), axis=1, keepdims=True)
    alive = (iota((group, capacity), 1).astype(F32) < counts).astype(F32)
    strength = drag_ref[0] * alive
    cell = cell_ref[0]
    rows = [strength * vel_ref[k, 0] for k in range(3)]
    rows.append(vol_ref[0] * alive)
    rows.append(weight_ref[0])
    rows.append(lax.rem(cell, size_z).astype(F32))
    rows.append(lax.div(cell, size_z).astype(F32))
    for k, row in enumerate(rows):
        payload[:, k, :] = row
    payload[:, 7, :] = rows[6]

    pl.semaphore_wait(barrier, group + 1)

    def payload_copy(offset):
        there_y, there_z = place(offset)
        return pltpu.make_async_remote_copy(
            src_ref=payload.at[there_y * n_z + there_z],
            dst_ref=arrived.at[offset],
            send_sem=pay_ssem.at[offset],
            recv_sem=pay_rsem.at[offset],
            device_id=(at_x, there_y, there_z),
            device_id_type=MESH,
        )

    def send_payload(offset, carry):
        payload_copy(offset).start()
        return carry

    lax.fori_loop(1, group, send_payload, 0)
    arrived[0] = payload[me]
    total[...] = jnp.zeros_like(total)

    width = STEP * capacity

    def chunk_rows(step):
        return jnp.concatenate([arrived[step * STEP + i] for i in range(STEP)], axis=1)

    def column_hot(slots):
        return (iota((columns, width), 0).astype(F32) == slots[6:7]).astype(F32).astype(BF16)

    def deposit(step, carry):
        for i in range(STEP):
            offset = step * STEP + i

            @pl.when(offset > 0)
            def _():
                payload_copy(offset).wait_recv()

        slots = chunk_rows(step)
        hot = column_hot(slots)
        level = iota((size_z, width), 0).astype(F32)
        here = level == slots[5:6]
        above = level == slots[5:6] + 1.0
        share = slots[4:5]
        highs, lows = [], []
        for k in range(4):
            first = split(slots[k : k + 1] * share)
            second = split(slots[k : k + 1] * (1.0 - share))
            for parts, a, b in ((highs, first[0], second[0]), (lows, first[1], second[1])):
                parts.append(jnp.where(here, a, jnp.where(above, b, 0.0)).astype(BF16))
        spread_high = jnp.concatenate(highs, axis=0)
        spread_low = jnp.concatenate(lows, axis=0)
        total[...] += dot(hot, spread_high, ((1,), (1,))) + dot(hot, spread_low, ((1,), (1,)))
        return carry

    lax.fori_loop(0, group // STEP, deposit, 0)

    faces = (
        (face_xs, face_xr, x_down, x_up),
        (face_ys, face_yr, y_down, y_up),
        (face_zs, face_zr, z_down, z_up),
    )

    def halo_copies(exchange, slot, fields, axis):
        sends, receives, down, up = faces[axis]
        return [
            pltpu.make_async_remote_copy(
                src_ref=sends.at[side, pl.ds(slot, fields)],
                dst_ref=receives.at[1 - side, pl.ds(slot, fields)],
                send_sem=halo_ssem.at[exchange, 2 * axis + side],
                recv_sem=halo_rsem.at[exchange, 2 * axis + 1 - side],
                device_id=there,
                device_id_type=MESH,
            )
            for side, there in ((0, down), (1, up))
        ]

    def start_halos(*which):
        for copy in halo_copies(*which):
            copy.start()

    def wait_halos(*which):
        for copy in halo_copies(*which):
            copy.wait_recv()

    inside = [
        jnp.where(flag, 1.0, 0.0)
        for flag in (at_x > 0, at_x < n_x - 1, at_y > 0, at_y < n_y - 1, at_z > 0, at_z < n_z - 1)
    ]
    rows_of = iota((LANES, size_z), 0)
    row_in = lax.rem(rows_of, size_y)
    lane_of = iota((LANES, size_z), 1)
    first_row, last_row = row_in == 0, row_in == size_y - 1
    first_lane, last_lane = lane_of == 0, lane_of == size_z - 1
    first_of_all, last_of_all = rows_of == 0, rows_of == LANES - 1
    ends_x = (pl.ds(0, size_y), pl.ds(columns - size_y, size_y))
    ends_x_pad = (pl.ds(size_y, size_y), pl.ds(columns, size_y))
    ends_y = (pl.ds(0, size_x, stride=size_y), pl.ds(size_y - 1, size_x, stride=size_y))
    ends_y_pad = (
        pl.ds(size_y, size_x, stride=size_y),
        pl.ds(2 * size_y - 1, size_x, stride=size_y),
    )
    signs = (-1.0, 1.0)

    def tile_rows(tile, shift=0):
        return pl.ds(pl.multiple_of(tile * LANES + shift * size_y, size_y), LANES)

    def each_tile(body):
        def step(tile, carry):
            body(tile)
            return carry

        lax.fori_loop(0, tiles, step, 0, unroll=UNROLL)

    def before(value, axis):
        return pltpu.roll(value, 1, axis)

    def after(value, axis):
        return pltpu.roll(value, value.shape[axis] - 1, axis)

    def pack(value):
        turned = value.T
        return turned[:1], turned[size_z - 1 :]

    def unpack(low, high):
        return jnp.where(first_of_all, low, jnp.where(last_of_all, high, 0.0)).T

    def put_z(slot, tile, value):
        for side, row in enumerate(pack(value)):
            face_zs[side, slot, pl.ds(tile, 1), :] = row

    back_copy.wait()

    zero_plane = jnp.zeros((size_y, size_z), F32)
    for rows in (pl.ds(0, size_y), pl.ds(columns + size_y, size_y)):
        mom_x[rows] = zero_plane
        porous[rows] = zero_plane
        press[0, rows] = zero_plane
        press[1, rows] = zero_plane

    def fields_step(tile):
        here = tile_rows(tile)
        along = [back[k, here] + total[here, k * size_z : (k + 1) * size_z] for k in range(3)]
        hollow = 1.0 / (1.0 + total[here, 3 * size_z :])
        mom_x[tile_rows(tile, 1)] = along[0]
        mom_y[here] = along[1]
        mom_z[here] = along[2]
        porous[tile_rows(tile, 1)] = hollow
        put_z(0, tile, along[2])
        put_z(1, tile, hollow)

    each_tile(fields_step)
    for side in range(2):
        face_xs[side, 0] = mom_x[ends_x_pad[side]]
        face_xs[side, 1] = porous[ends_x_pad[side]]
    start_halos(0, 0, 2, 0)
    start_halos(0, 0, 2, 2)
    for side in range(2):
        face_ys[side, 0] = mom_y[ends_y[side]]
        face_ys[side, 1] = porous[ends_y_pad[side]]
    start_halos(0, 0, 2, 1)

    def weights_step(tile):
        here = tile_rows(tile)
        centre = porous[tile_rows(tile, 1)]
        half = 0.5 * centre
        coef[0, here] = half + 0.5 * porous[tile_rows(tile, 2)]
        coef[1, here] = half + 0.5 * porous[tile_rows(tile)]
        whole = coef[0, here] + coef[1, here]
        source = mom_x[tile_rows(tile, 2)] - mom_x[tile_rows(tile)]
        for k, axis, value, last, first in (
            (2, 0, mom_y[here], last_row, first_row),
            (4, 1, mom_z[here], last_lane, first_lane),
        ):
            up = half + 0.5 * after(centre, axis)
            down = half + 0.5 * before(centre, axis)
            coef[k, here] = jnp.where(last, 0.0, up)
            coef[k + 1, here] = jnp.where(first, 0.0, down)
            whole = whole + jnp.where(last, half, up) + jnp.where(first, half, down)
            source = source + jnp.where(last, 0.0, after(value, axis))
            source = source - jnp.where(first, 0.0, before(value, axis))
        coef[6, here] = 0.5 * source
        diagonal[here] = whole

    each_tile(weights_step)

    def outside(side, value):
        return value * inside[side] + (1.0 - inside[side])

    wait_halos(0, 0, 2, 2)
    beyond = [outside(4 + side, face_zr[side, 1]) for side in range(2)]
    for side in range(2):
        edge_z[side] = 0.5 * (face_zs[side, 1] + beyond[side])
        work_z[side] = 0.5 * beyond[side]
        work_z[2 + side] = (0.5 * signs[side]) * inside[4 + side] * face_zr[side, 0]

    def halo_z_step(tile):
        here = tile_rows(tile)
        row = pl.ds(tile, 1)
        diagonal[here] += unpack(work_z[0, row], work_z[1, row])
        coef[6, here] += unpack(work_z[2, row], work_z[3, row])

    each_tile(halo_z_step)
    wait_halos(0, 0, 2, 1)
    for side in range(2):
        value = outside(2 + side, face_yr[side, 1])
        edge_y[side] = 0.5 * (face_ys[side, 1] + value)
        diagonal[ends_y[side]] += 0.5 * value
        source_y = (0.5 * signs[side]) * inside[2 + side] * face_yr[side, 0]
        coef[6, ends_y[side]] += source_y
    wait_halos(0, 0, 2, 0)
    for side in range(2):
        value = outside(side, face_xr[side, 1])
        edge_x[side] = 0.5 * (face_xs[side, 1] + value)
        diagonal[ends_x[side]] += 0.5 * value
        coef[6, ends_x[side]] += (0.5 * signs[side]) * inside[side] * face_xr[side, 0]

    def send_x(exchange, slot, buffer):
        for side in range(2):
            face_xs[side, slot] = press[buffer, ends_x_pad[side]]
        start_halos(exchange, slot, 1, 0)

    def send_y(exchange, slot, buffer):
        for side in range(2):
            face_ys[side, slot] = press[buffer, ends_y_pad[side]]
        start_halos(exchange, slot, 1, 1)

    def first_step(tile):
        here = tile_rows(tile)
        inverse = 1.0 / diagonal[here]
        scaled = coef[6, here] * inverse
        diagonal[here] = inverse
        coef[6, here] = scaled
        press[1, tile_rows(tile, 1)] = -scaled
        put_z(2, tile, -scaled)

    each_tile(first_step)
    send_x(1, 2, 1)
    start_halos(1, 2, 1, 2)
    send_y(1, 2, 1)

    def scale_step(tile):
        here = tile_rows(tile)
        inverse = diagonal[here]
        for k in range(6):
            coef[k, here] *= inverse
        for side, row in enumerate(pack(inverse)):
            work_z[side, pl.ds(tile, 1)] = row

    each_tile(scale_step)
    for side in range(2):
        edge_x[side] *= diagonal[ends_x[side]] * inside[side]
        edge_y[side] *= diagonal[ends_y[side]] * inside[2 + side]
        edge_z[side] *= work_z[side] * inside[4 + side]

    def sweep(exchange, carry):
        old = lax.rem(exchange, 2)
        new = 1 - old
        slot = exchange + 1

        def inner_step(tile):
            here = tile_rows(tile)
            centre = press[old, tile_rows(tile, 1)]
            value = coef[0, here] * press[old, tile_rows(tile, 2)]
            value = value + coef[1, here] * press[old, tile_rows(tile)]
            for k, axis in ((2, 0), (4, 1)):
                value = value + coef[k, here] * after(centre, axis)
                value = value + coef[k + 1, here] * before(centre, axis)
            press[new, tile_rows(tile, 1)] = value - coef[6, here]

        each_tile(inner_step)
        wait_halos(exchange, slot, 1, 2)
        for side in range(2):
            work_z[side] = edge_z[side] * face_zr[side, slot]

        def side_z_step(tile):
            row = pl.ds(tile, 1)
            press[new, tile_rows(tile, 1)] += unpack(work_z[0, row], work_z[1, row])

        each_tile(side_z_step)
        wait_halos(exchange, slot, 1, 1)
        for side in range(2):
            press[new, ends_y_pad[side]] += edge_y[side] * face_yr[side, slot]

        each_tile(lambda tile: put_z(slot + 1, tile, press[new, tile_rows(tile, 1)]))
        wait_halos(exchange, slot, 1, 0)
        for side in range(2):
            press[new, ends_x_pad[side]] += edge_x[side] * face_xr[side, slot]
        send_x(exchange + 1, slot + 1, new)
        for tile in (0, tiles - 1):
            put_z(slot + 1, tile, press[new, tile_rows(tile, 1)])
        start_halos(exchange + 1, slot + 1, 1, 2)
        send_y(exchange + 1, slot + 1, new)
        return carry

    lax.fori_loop(1, SWEEPS, sweep, 0)

    last = SWEEPS % 2
    slot = SWEEPS + 1

    def put_velocity(k, rows, where, value):
        high, low = split(value)
        vel_t[pl.ds(k * size_z + rows.start, rows.size), where] = high.astype(BF16)
        vel_t[pl.ds((3 + k) * size_z + rows.start, rows.size), where] = low.astype(BF16)

    all_z = pl.ds(0, size_z)

    def velocity_step(tile):
        here = tile_rows(tile)
        centre = press[last, tile_rows(tile, 1)]
        pressure_ref[here] = centre
        hollow = porous[tile_rows(tile, 1)]
        slope = press[last, tile_rows(tile, 2)] - press[last, tile_rows(tile)]
        value = hollow * (mom_x[tile_rows(tile, 1)] - 0.5 * slope)
        mom_x[tile_rows(tile, 1)] = value
        put_velocity(0, all_z, here, value.T)
        high = jnp.where(last_row, 0.0, after(centre, 0))
        low = jnp.where(first_row, 0.0, before(centre, 0))
        mom_y[here] = hollow * (mom_y[here] - 0.5 * (high - low))
        high = jnp.where(last_lane, 0.0, after(centre, 1))
        low = jnp.where(first_lane, 0.0, before(centre, 1))
        value = (hollow * (mom_z[here] - 0.5 * (high - low))).T
        put_velocity(2, all_z, here, value)
        edge_v[0, :, here] = value[:16]
        edge_v[1, :, here] = value[size_z - 16 :]

    each_tile(velocity_step)
    wait_halos(SWEEPS, slot, 1, 1)
    for side in range(2):
        mom_y[ends_y[side]] -= (0.5 * signs[side]) * inside[2 + side] * (
            face_ys[side, 1] * face_yr[side, slot]
        )
    each_tile(lambda tile: put_velocity(1, all_z, tile_rows(tile), mom_y[tile_rows(tile)].T))
    wait_halos(SWEEPS, slot, 1, 2)
    for side in range(2):
        work_z[side] = (-0.5 * signs[side]) * inside[4 + side] * (
            face_zs[side, 1] * face_zr[side, slot]
        )
    block_row = iota((16, LANES), 0)
    for side in range(2):
        for tile in range(tiles):
            here = pl.ds(tile * LANES, LANES)
            fix = jnp.where(block_row == 15 * side, work_z[side, tile : tile + 1], 0.0)
            rows = pl.ds((size_z - 16) * side, 16)
            put_velocity(2, rows, here, edge_v[side, :, here] + fix)
    wait_halos(SWEEPS, slot, 1, 0)
    for side in range(2):
        mom_x[ends_x_pad[side]] -= (0.5 * signs[side]) * inside[side] * (
            porous[ends_x_pad[side]] * face_xr[side, slot]
        )
    for tile in (0, tiles - 1):
        put_velocity(0, all_z, pl.ds(tile * LANES, LANES), mom_x[tile_rows(tile, 1)].T)

    def return_copy(offset):
        there_y, there_z = place_back(offset)
        return pltpu.make_async_remote_copy(
            src_ref=picked.at[offset],
            dst_ref=returned.at[me],
            send_sem=ret_ssem.at[offset],
            recv_sem=ret_rsem.at[offset],
            device_id=(at_x, there_y, there_z),
            device_id_type=MESH,
        )

    def pick(turn, carry):
        step = group // STEP - 1 - turn
        slots = chunk_rows(step)
        both = dot(vel_t[...], column_hot(slots), ((1,), (0,)))
        level = iota((size_z, width), 0).astype(F32)
        share = slots[4:5]
        reach = jnp.where(
            level == slots[5:6], share, jnp.where(level == slots[5:6] + 1.0, 1.0 - share, 0.0)
        )
        found = []
        for k in range(3):
            value = (
                both[k * size_z : (k + 1) * size_z] + both[(3 + k) * size_z : (4 + k) * size_z]
            )
            found.append(jnp.sum(value * reach, axis=0, keepdims=True))
        found.append(jnp.zeros_like(found[0]))
        found = jnp.concatenate(found, axis=0)
        for i in range(STEP):
            offset = step * STEP + i
            picked[offset] = found[:, i * capacity : (i + 1) * capacity]

            @pl.when(offset > 0)
            def _():
                return_copy(offset).start()

        return carry

    lax.fori_loop(0, group // STEP, pick, 0)
    returned[me] = picked[0]

    def finish(offset, carry):
        copy = return_copy(offset)
        copy.wait_recv()
        copy.wait_send()
        payload_copy(offset).wait_send()
        return carry

    lax.fori_loop(1, group, finish, 0)
    for k in range(3):
        slots_ref[k, 0] = returned[:, k, :] * alive

    def finish_halos(exchange, carry):
        for axis in range(3):
            for copy in halo_copies(exchange, exchange + 1, 1, axis):
                copy.wait_send()
        return carry

    for axis in range(3):
        for copy in halo_copies(0, 0, 2, axis):
            copy.wait_send()
    lax.fori_loop(1, SWEEPS + 1, finish_halos, 0)


def store_kernel(pressure_ref, slots_ref, pressure_out, slots_out, sems):
    copies = [
        pltpu.make_async_copy(pressure_ref, pressure_out, sems.at[0]),
        pltpu.make_async_copy(slots_ref, slots_out, sems.at[1]),
    ]
    for copy in copies:
        copy.start()
    for copy in copies:
        copy.wait()


def per_device(sizes, *args):
    vel, drag = args[0], args[1]
    back = args[6]
    group, capacity = drag.shape[1:]
    _, size_x, size_y, size_z = back.shape
    columns = size_x * size_y
    tile_rows = columns // LANES
    slots = SWEEPS + 2
    vmem = pl.BlockSpec(memory_space=pltpu.VMEM)
    field = pltpu.VMEM((columns, size_z), F32)
    padded = pltpu.VMEM((columns + 2 * size_y, size_z), F32)
    dma = pltpu.SemaphoreType.DMA
    pressure, slot_velocity = pl.pallas_call(
        functools.partial(step_kernel, sizes),
        out_shape=(
            jax.ShapeDtypeStruct((columns, size_z), F32),
            jax.ShapeDtypeStruct(vel.shape, F32),
        ),
        in_specs=[vmem] * 6 + [pl.BlockSpec(memory_space=pl.ANY)],
        out_specs=(vmem, vmem),
        scratch_shapes=[
            pltpu.VMEM((3, columns, size_z), F32),
            pltpu.VMEM((group, 8, capacity), F32),
            pltpu.VMEM((group, 8, capacity), F32),
            pltpu.VMEM((columns, 4 * size_z), F32),
            padded,
            field,
            field,
            padded,
            pltpu.VMEM((7, columns, size_z), F32),
            pltpu.VMEM((2, columns + 2 * size_y, size_z), F32),
            field,
            pltpu.VMEM((2, size_y, size_z), F32),
            pltpu.VMEM((2, size_x, size_z), F32),
            pltpu.VMEM((2, tile_rows, LANES), F32),
            pltpu.VMEM((4, tile_rows, LANES), F32),
            pltpu.VMEM((2, 16, columns), F32),
            pltpu.VMEM((6 * size_z, columns), BF16),
            pltpu.VMEM((group, 4, capacity), F32),
            pltpu.VMEM((group, 4, capacity), F32),
            pltpu.VMEM((2, slots, size_y, size_z), F32),
            pltpu.VMEM((2, slots, size_y, size_z), F32),
            pltpu.VMEM((2, slots, size_x, size_z), F32),
            pltpu.VMEM((2, slots, size_x, size_z), F32),
            pltpu.VMEM((2, slots, tile_rows, LANES), F32),
            pltpu.VMEM((2, slots, tile_rows, LANES), F32),
            dma,
            dma((group,)),
            dma((group,)),
            dma((group,)),
            dma((group,)),
            dma((SWEEPS + 1, 6)),
            dma((SWEEPS + 1, 6)),
        ],
        compiler_params=pltpu.CompilerParams(
            collective_id=0, has_side_effects=True, vmem_limit_bytes=56 * 2**20
        ),
    )(*args[:6], back.reshape(3, columns, size_z))
    anywhere = pl.BlockSpec(memory_space=pl.ANY)
    pressure, slot_velocity = pl.pallas_call(
        store_kernel,
        out_shape=(
            jax.ShapeDtypeStruct(pressure.shape, F32),
            jax.ShapeDtypeStruct(slot_velocity.shape, F32),
        ),
        in_specs=[vmem, vmem],
        out_specs=(anywhere, anywhere),
        scratch_shapes=[dma((2,))],
    )(pressure, slot_velocity)
    return pressure.reshape(size_x, size_y, size_z), slot_velocity


def solution(mesh):
    sizes = (mesh.shape["gx"], mesh.shape["gy"], mesh.shape["gz"])
    block = ("gx", "gy", "gz")
    return jax.shard_map(
        functools.partial(per_device, sizes),
        mesh=mesh,
        in_specs=(
            P(None, block, None, None),
            P(block, None, None),
            P(block, None, None),
            P(block, None, None),
            P(block, None, None),
            P(block, None),
            P(None, *block),
        ),
        out_specs=(P(*block), P(None, block, None, None)),
        check_vma=False,
    )
```
